256 devices in a mesh: replica: 4 (over x_lo, core), fsdp: 64 (over z, y, x_hi).
Axes of the slice: x: 4 (x_hi: 2, x_lo: 2; x = x_hi * 2 + x_lo), y: 4, z: 8, core: 2. Of those that a mesh axis runs over, the one named last changes fastest.
Arguments:
- global_frag: float32 [2048, 8192], P('fsdp'), may hold values from -6 to 6
- local_frag: float32 [4, 2048, 8192], P('replica', 'fsdp'), may hold values from -6 to 6
- outer_mom: float32 [2048, 8192], P('fsdp'), may hold values from -6 to 6
- grads: bfloat16 [4, 64, 256, 8192], P('replica', 'fsdp'), may hold values from -512 to 512
- inner_param: float32 [4, 256, 8192], P('replica', 'fsdp'), may hold values from -6 to 6
- inner_m: float32 [4, 256, 8192], P('replica', 'fsdp'), may hold values from -6 to 6
- inner_v: float32 [4, 256, 8192], P('replica', 'fsdp'), may hold values from 0.05 to 4
Outputs:
- new_global: float32 [2048, 8192], P('fsdp')
- new_mom: float32 [2048, 8192], P('fsdp')
- new_param: float32 [4, 256, 8192], P('replica', 'fsdp')
- new_m: float32 [4, 256, 8192], P('replica', 'fsdp')
- new_v: float32 [4, 256, 8192], P('replica', 'fsdp')
The draws below stay inside these ranges and needn't reach their ends.
All inputs are finite; a program needn't handle non-finite values.
Results may differ from the reference program's by a relative error of at most 0.0065.
Values may be sent and summed in bfloat16 or wider, within the bound.
No kernel may reach another device: no remote copies, remote signals or barrier semaphores. Data moves between devices by JAX's collectives and lax.ppermute only.
A program may use at most 128 MiB of HBM per device.

```python
import math
import jax
import jax.numpy as jnp
from jax import lax

D = 8192
BLOCK = 128
STEP = 8
FRAG = 2048
BUCKET = 256
N_REPLICA = 4
N_FSDP = 64


def with_spikes(entries, key, source, target, blocks, factor):
    owner, partner = [(jnp.arange(entries.shape[axis_at]) // (entries.shape[axis_at] // blocks)).reshape([-1 if axis == axis_at else 1 for axis in range(entries.ndim)]) for axis_at in (source, target)]
    chosen = jax.random.permutation(key, blocks)[partner]
    strong = (owner == chosen) | (owner == (partner + blocks // 2) % blocks)
    return jnp.where(strong, factor * entries, entries)


def steps_of(own_key, extent, pieces, least, largest):
    def one(dim, shards_of):
        steps = jax.random.uniform(jax.random.fold_in(jax.random.fold_in(own_key, 6), dim), (shards_of,), jnp.float32, least / len(pieces), largest / len(pieces))
        return jnp.repeat(jnp.exp(steps), extent[dim] // shards_of).reshape((-1,) + (1,) * (len(extent) - dim - 1))

    level = one(*pieces[0])
    for cut in pieces[1:]:
        level = level * one(*cut)
    return level


def normal_values(own_key, dims, spread, limit, split=(), held_as=jnp.bfloat16):
    result = jax.random.normal(own_key, dims, jnp.float32) * spread
    if len(split) > 0:
        result = steps_of(own_key, dims, split, -0.22, 0.18) * result
    return jnp.clip(result, min=-limit, max=limit).astype(held_as)


def heavy_noise(own_key, shape, scale, bound, cuts, heavy, kind=jnp.bfloat16):
    values = scale * jax.random.normal(own_key, shape, jnp.float32)
    if cuts:
        values = values * steps_of(own_key, shape, cuts, -0.22, 0.18)
    return jnp.clip(with_spikes(values, jax.random.fold_in(own_key, 3), *heavy), -bound, bound).astype(kind)


def setup_inputs(seed: int = 0) -> dict:
    key_of = jax.random.split(jax.random.key(seed), 8)
    global_frag = normal_values(key_of[0], (FRAG, D), 1.0, 6.0, ((0, 64),), jnp.float32)
    local_frag = normal_values(key_of[1], (N_REPLICA, FRAG, D), 1.0, 6.0, ((0, 4), (1, 64)), jnp.float32)
    outer_mom = normal_values(key_of[2], (FRAG, D), 1.0, 6.0, ((0, 64),), jnp.float32)
    grads = heavy_noise(key_of[3], (N_REPLICA, N_FSDP, BUCKET, D), 32.0, 512.0, ((0, 4), (1, 64)), (1, 2, 64, 4.0))
    inner_param = normal_values(key_of[4], (N_REPLICA, BUCKET, D), 1.0, 6.0, ((0, 4), (1, 64)), jnp.float32)
    inner_m = normal_values(key_of[5], (N_REPLICA, BUCKET, D), 1.0, 6.0, ((0, 4), (1, 64)), jnp.float32)
    inner_v = jnp.clip(jnp.exp(math.log(4.0) - 4.3820266 * jax.random.uniform(key_of[6], (N_REPLICA, BUCKET, D), jnp.float32) ** steps_of(key_of[6], (N_REPLICA, BUCKET, D), ((0, 4), (1, 64)), -0.2, 0.2)), 0.05, 4.0)
    return dict(global_frag=global_frag, local_frag=local_frag, outer_mom=outer_mom, grads=grads, inner_param=inner_param, inner_m=inner_m, inner_v=inner_v)


def reference(global_frag, local_frag, outer_mom, grads, inner_param, inner_m, inner_v):
    delta = global_frag[None] - local_frag
    blocks = delta.reshape(delta.shape[0], delta.shape[1], D // BLOCK, BLOCK)
    amax = lax.optimization_barrier(jnp.max(jnp.abs(blocks), axis=-1))
    scale = ((amax + 1e-06) / 448.0).astype(jnp.bfloat16)
    scale_wide = scale.astype(jnp.float32)[..., None]
    encoded = (blocks / scale_wide).astype(jnp.bfloat16)
    decoded = encoded.astype(jnp.float32) * scale_wide
    average = (0.25 * lax.optimization_barrier(jnp.sum(decoded, axis=0))).reshape(global_frag.shape)
    new_mom = 0.9 * outer_mom + average
    new_global = global_frag - 0.7 * (average + 0.9 * new_mom)
    gmean = lax.optimization_barrier(jnp.sum(grads, axis=1, dtype=jnp.float32)) / N_FSDP
    new_m = 0.9 * inner_m + 0.1 * gmean
    new_v = 0.95 * inner_v + 0.05 * gmean * gmean
    m_hat = new_m / (1.0 - 0.9 ** STEP)
    v_hat = new_v / (1.0 - 0.95 ** STEP)
    new_param = inner_param - 0.0003 * (m_hat / (jnp.sqrt(v_hat) + 1e-08) + 0.1 * inner_param)
    return (new_global, new_mom, new_param, new_m, new_v)
```

```python
import jax
import jax.numpy as jnp
from jax import lax
from jax.sharding import PartitionSpec as P

BLOCK = 128
STEP = 8
NZ, NY, NH = 8, 4, 2
F32, F16, BF16 = jnp.float32, jnp.float16, jnp.bfloat16
COLS_Y, COLS_H, COLS_Z = 2816, 2816, 2560
FRAG_SCALE = 2048.0


def place(z, y, h):
    return ((z % NZ) * NY + y % NY) * NH + h % NH


def perm_of(step):
    return [
        (place(z, y, h), place(*step(z, y, h)))
        for z in range(NZ)
        for y in range(NY)
        for h in range(NH)
    ]


def along_y(x, k):
    return lax.ppermute(x, "fsdp", perm_of(lambda z, y, h: (z, y + k, h)))


def along_h(x):
    return lax.ppermute(x, "fsdp", perm_of(lambda z, y, h: (z, y, h + 1)))


def along_z(x, k):
    return lax.ppermute(x, "fsdp", perm_of(lambda z, y, h: (z + k, y, h)))


def pair_z(x, shift):
    return lax.ppermute(
        x, "fsdp", perm_of(lambda z, y, h: ((((z + shift) % NZ) ^ 1) - shift, y, h))
    )


def take(x, index, axis):
    return lax.dynamic_index_in_dim(x, index, axis, keepdims=False)


def rows_of(x, h, axis):
    low = lax.slice_in_dim(x, 0, 4, axis=axis)
    high = lax.slice_in_dim(x, 4, 8, axis=axis)
    return jnp.where(h == 0, low, high)


def direct(x, me, size, axis, send, factor):
    parts = [
        send(take(x, lax.rem(me + k, size), axis).astype(F16), k) for k in range(1, size)
    ]
    total = take(x, me, axis).astype(F32)
    for part in parts:
        total = total + part.astype(F32)
    return total * factor


def bucket_sum(g, f):
    z, y, h = f // (NY * NH), (f // NH) % NY, f % NH
    p, j = z % 2, z // 2
    g = g.reshape(NZ, NY, 8, g.shape[-1])
    ga = g[..., :COLS_Y]
    gc = g[..., COLS_Y : COLS_Y + COLS_H]
    gb = g[..., COLS_Y + COLS_H :].reshape(NZ // 2, 2, NY, 8, COLS_Z)
    c_part = along_h(rows_of(gc, 1 - h, 2))
    b_part = pair_z(take(gb, 1 - p, 1), 0)
    a_parts = [along_y(take(ga, lax.rem(y + k, NY), 1), k) for k in range(1, NY)]
    a = take(ga, y, 1).astype(F32)
    for part in a_parts:
        a = a + part.astype(F32)
    a = (a * 16.0).reshape(NZ // 2, 2, 8, COLS_Y)
    c = (rows_of(gc, h, 2).astype(F32) + c_part.astype(F32)) * 32.0
    b = (take(gb, p, 1).astype(F32) + b_part.astype(F32)) * 32.0
    a_part = pair_z(take(a, 1 - p, 1).astype(F16), 0)
    b_part = along_h(rows_of(b, 1 - h, 2).astype(F16))
    a = (take(a, p, 1) + a_part.astype(F32)) * 0.5
    b = (rows_of(b, h, 2) + b_part.astype(F32)) * 0.5
    c = direct(c, y, NY, 1, along_y, 0.25).reshape(NZ // 2, 2, 4, COLS_H)
    a_part = along_h(rows_of(a, 1 - h, 1).astype(F16))
    c_part = pair_z(take(c, 1 - p, 1).astype(F16), 0)
    a = (rows_of(a, h, 1) + a_part.astype(F32)) * 0.5
    c = (take(c, p, 1) + c_part.astype(F32)) * 0.5
    b = direct(b, y, NY, 1, along_y, 0.25)
    ac = jnp.concatenate([a, c], axis=-1)
    t = jnp.concatenate([ac, b], axis=-1)
    return direct(t, j, NZ // 2, 0, lambda x, k: along_z(x, 2 * k), 0.25)


def fragment_total(delta, r):
    rows, width = delta.shape
    blocks = delta.reshape(rows, width // BLOCK, BLOCK)
    amax = jnp.max(jnp.abs(blocks), axis=-1)
    scale = ((amax + 1e-06) / 448.0).astype(BF16).astype(F32)[..., None]
    encoded = (blocks / scale).astype(BF16)
    decoded = (encoded.astype(F32) * scale).reshape(2, rows // 2, width)
    core = r % 2
    swap_core = [(0, 1), (1, 0), (2, 3), (3, 2)]
    swap_chip = [(0, 2), (2, 0), (1, 3), (3, 1)]
    other = lax.ppermute(take(decoded, 1 - core, 0), "replica", swap_core)
    pair = ((take(decoded, core, 0) + other) * FRAG_SCALE).astype(F16)
    far = lax.ppermute(pair, "replica", swap_chip)
    mine = (pair.astype(F32) + far.astype(F32)) * (1.0 / FRAG_SCALE)
    theirs = lax.ppermute(mine, "replica", swap_core)
    low = jnp.where(core == 0, mine, theirs)
    high = jnp.where(core == 0, theirs, mine)
    return jnp.concatenate([low, high], axis=0)


def on_device(global_frag, local_frag, outer_mom, grads, inner_param, inner_m, inner_v):
    f = lax.axis_index("fsdp")
    r = lax.axis_index("replica")
    groups = lax.axis_size("fsdp")
    summed = bucket_sum(grads[0, 0], f)
    total = fragment_total(global_frag - local_frag[0], r)
    average = 0.25 * total
    new_mom = 0.9 * outer_mom + average
    new_global = global_frag - 0.7 * (average + 0.9 * new_mom)
    gmean = (summed / groups)[None]
    new_m = 0.9 * inner_m + 0.1 * gmean
    new_v = 0.95 * inner_v + 0.05 * gmean * gmean
    m_hat = new_m / (1.0 - 0.9**STEP)
    v_hat = new_v / (1.0 - 0.95**STEP)
    new_param = inner_param - 0.0003 * (m_hat / (jnp.sqrt(v_hat) + 1e-08) + 0.1 * inner_param)
    return (new_global, new_mom, new_param, new_m, new_v)


def solution(mesh):
    placed = (
        P("fsdp", None),
        P("replica", "fsdp", None),
        P("fsdp", None),
        P("replica", "fsdp", None, None),
        P("replica", "fsdp", None),
        P("replica", "fsdp", None),
        P("replica", "fsdp", None),
    )
    return jax.shard_map(
        on_device,
        mesh=mesh,
        in_specs=placed,
        out_specs=(
            P("fsdp", None),
            P("fsdp", None),
            P("replica", "fsdp", None),
            P("replica", "fsdp", None),
            P("replica", "fsdp", None),
        ),
        check_vma=False,
    )
```

```python
import jax
import jax.numpy as jnp
from jax import lax
from jax.experimental import pallas as pl
from jax.experimental.pallas import tpu as pltpu
from jax.sharding import PartitionSpec as P

BLOCK = 128
STEP = 8
NZ, NY, NH = 8, 4, 2
F32, F16, BF16 = jnp.float32, jnp.float16, jnp.bfloat16
COLS_Y, COLS_H, COLS_Z = 3072, 2560, 2560
FRAG_SCALE = 2048.0


def place(z, y, h):
    return ((z % NZ) * NY + y % NY) * NH + h % NH


def perm_of(step):
    return [
        (place(z, y, h), place(*step(z, y, h)))
        for z in range(NZ)
        for y in range(NY)
        for h in range(NH)
    ]


def along_y(x, k):
    return lax.ppermute(x, "fsdp", perm_of(lambda z, y, h: (z, y + k, h)))


def along_h(x):
    return lax.ppermute(x, "fsdp", perm_of(lambda z, y, h: (z, y, h + 1)))


def along_z(x, k):
    return lax.ppermute(x, "fsdp", perm_of(lambda z, y, h: (z + k, y, h)))


def pair_z(x, shift):
    return lax.ppermute(
        x, "fsdp", perm_of(lambda z, y, h: ((((z + shift) % NZ) ^ 1) - shift, y, h))
    )


def swap_core(x):
    return lax.ppermute(x, "replica", [(0, 1), (1, 0), (2, 3), (3, 2)])


def take(x, index, axis):
    return lax.dynamic_index_in_dim(x, index, axis, keepdims=False)


def rows_of(x, h, axis):
    low = lax.slice_in_dim(x, 0, 4, axis=axis)
    high = lax.slice_in_dim(x, 4, 8, axis=axis)
    return jnp.where(h == 0, low, high)


def spread(x, me, size, axis):
    others = [take(x, lax.rem(me + k, size), axis).astype(F16) for k in range(1, size)]
    return take(x, me, axis), others


def gather(x, parts, factor):
    for part in parts:
        x = x + part.astype(F32)
    return x * factor


def decode(g, l, mine, theirs):
    core = lax.rem(lax.axis_index("replica"), 2)
    half = g.shape[0] // 2
    for i in range(g.shape[1] // BLOCK):
        at = slice(i * BLOCK, (i + 1) * BLOCK)
        delta = g[:, at] - l[:, at]
        amax = jnp.max(jnp.abs(delta), axis=1, keepdims=True)
        scale = ((amax + 1e-06) / 448.0).astype(BF16).astype(F32)
        decoded = (delta / scale) * scale
        low, high = decoded[:half], decoded[half:]
        mine[:, at] = jnp.where(core == 0, low, high)
        theirs[:, at] = jnp.where(core == 0, high, low)


def deal_kernel(
    g, frag_g, frag_l, a1, a2, a3, a0, c_send, c_own, b_send, b_own, mine_out, theirs_out, *scratch
):
    c_all, c_s, c_o, fg, fl, mine, theirs, a_all, b_all, sems = scratch
    f = lax.axis_index("fsdp")
    y, h, p = lax.rem(f // NH, NY), lax.rem(f, NH), lax.rem(f // (NY * NH), 2)
    first, second = COLS_Y, COLS_Y + COLS_H

    def start(src, dst, i):
        copy = pltpu.make_async_copy(src, dst, sems.at[i])
        copy.start()
        return copy

    fg_in = start(frag_g, fg, 0)
    fl_in = start(frag_l, fl, 1)
    a_in = [start(g.at[:, :, lax.rem(y + k, NY), :, :first], a_all.at[k], 2 + k) for k in range(NY)]
    b_in = [start(g.at[:, q, :, :, second:], b_all.at[i], 6 + i) for i, q in enumerate((1 - p, p))]
    c_in = start(g.at[:, :, :, :, first:second], c_all, 8)
    fg_in.wait()
    fl_in.wait()
    decode(fg, fl, mine, theirs)
    dealt = [start(mine, mine_out, 9), start(theirs, theirs_out, 10)]
    for k, out in enumerate((a0, a1, a2, a3)):
        a_in[k].wait()
        dealt.append(start(a_all.at[k], out, 11 + k))
    for i, out in enumerate((b_send, b_own)):
        b_in[i].wait()
        dealt.append(start(b_all.at[i], out, 15 + i))
    c_in.wait()
    for i in range(NZ // 2):
        for q in range(2):
            for j in range(NY):
                low, high = c_all[i, q, j, 0:4, :], c_all[i, q, j, 4:8, :]
                c_s[i, q, j] = jnp.where(h == 0, high, low)
                c_o[i, q, j] = jnp.where(h == 0, low, high)
    dealt.append(start(c_s, c_send, 17))
    dealt.append(start(c_o, c_own, 18))
    for copy in dealt:
        copy.wait()


def deal(g, frag_g, frag_l):
    rows, width = frag_g.shape
    a = jax.ShapeDtypeStruct((NZ // 2, 2, 8, COLS_Y), BF16)
    b = jax.ShapeDtypeStruct((NZ // 2, NY, 8, COLS_Z), BF16)
    c = jax.ShapeDtypeStruct((NZ // 2, 2, NY, 4, COLS_H), BF16)
    half = jax.ShapeDtypeStruct((rows // 2, width), F32)
    anywhere = pl.BlockSpec(memory_space=pl.ANY)
    hbm = pl.BlockSpec(memory_space=pltpu.HBM)
    return pl.pallas_call(
        deal_kernel,
        out_shape=(a, a, a, a, c, c, b, b, half, half),
        in_specs=[hbm] * 3,
        out_specs=(anywhere,) * 10,
        scratch_shapes=[
            pltpu.VMEM((NZ // 2, 2, NY, 8, COLS_H), BF16),
            pltpu.VMEM((NZ // 2, 2, NY, 4, COLS_H), BF16),
            pltpu.VMEM((NZ // 2, 2, NY, 4, COLS_H), BF16),
            pltpu.VMEM((rows, width), F32),
            pltpu.VMEM((rows, width), F32),
            pltpu.VMEM((rows // 2, width), F32),
            pltpu.VMEM((rows // 2, width), F32),
            pltpu.VMEM((NY, NZ // 2, 2, 8, COLS_Y), BF16),
            pltpu.VMEM((2, NZ // 2, NY, 8, COLS_Z), BF16),
            pltpu.SemaphoreType.DMA((19,)),
        ],
        compiler_params=pltpu.CompilerParams(vmem_limit_bytes=18 << 20),
        cost_estimate=pl.CostEstimate(
            flops=8 * rows * width, bytes_accessed=12 << 20, transcendentals=0
        ),
    )(*(pltpu.with_memory_space_constraint(x, pltpu.HBM) for x in (g, frag_g, frag_l)))


def sums(g, frag, f):
    z, y, h = f // (NY * NH), (f // NH) % NY, f % NH
    p, j = z % 2, z // 2
    a1, a2, a3, a0, c_send, c_own, b_send, b_own, mine, theirs = deal(
        g.reshape(NZ // 2, 2, NY, 8, g.shape[-1]), *frag
    )
    together = lax.optimization_barrier
    a_parts = [along_y(a2, 2), along_y(a1, 1), along_y(a3, 3)]
    c_part = along_h(c_send)
    b_part = pair_z(b_send, 0)
    near = swap_core(theirs)
    pair = ((mine + near) * FRAG_SCALE).astype(F16)
    a0, c_own, b_own, a_parts, c_part, b_part = together(
        (a0, c_own, b_own, a_parts, c_part, b_part)
    )
    a = a0.astype(F32)
    for part in a_parts:
        a = a + part.astype(F32)
    a = a * 16.0
    b = (b_own.astype(F32) + b_part.astype(F32)) * 32.0
    c = (c_own.astype(F32) + c_part.astype(F32)) * 32.0
    a, a_send = rows_of(a, h, 2), rows_of(a, 1 - h, 2).astype(F16)
    b, b_sends = spread(b, y, NY, 1)
    c, c_send = take(c, p, 1), take(c, 1 - p, 1).astype(F16)
    a, a_send, b, b_sends, c, c_send = together((a, a_send, b, b_sends, c, c_send))
    b_parts = [along_y(b_sends[k - 1], k) for k in (2, 1, 3)]
    a_part = along_h(a_send)
    far = lax.ppermute(pair, "replica", [(0, 2), (2, 0), (1, 3), (3, 1)])
    c_part = pair_z(c_send, 0)
    a, a_part, b, b_parts, c, c_part, pair, far = together(
        (a, a_part, b, b_parts, c, c_part, pair, far)
    )
    a = (a + a_part.astype(F32)) * 0.5
    b = gather(b, b_parts, 0.25)
    c = (c + c_part.astype(F32)) * 0.5
    mine = (pair.astype(F32) + far.astype(F32)) * (1.0 / FRAG_SCALE)
    a, a_send = take(a, p, 1), take(a, 1 - p, 1).astype(F16)
    b, b_send = rows_of(b, h, 1), rows_of(b, 1 - h, 1).astype(F16)
    c, c_sends = spread(c, y, NY, 1)
    a, a_send, b, b_send, c, c_sends, mine = together(
        (a, a_send, b, b_send, c, c_sends, mine)
    )
    theirs = swap_core(mine)
    c_parts = [along_y(c_sends[k - 1], k) for k in (2, 1, 3)]
    b_part = along_h(b_send)
    a_part = pair_z(a_send, 0)
    a, a_part, b, b_part, c, c_parts, mine, theirs = together(
        (a, a_part, b, b_part, c, c_parts, mine, theirs)
    )
    a = (a + a_part.astype(F32)) * 0.5
    b = (b + b_part.astype(F32)) * 0.5
    c = gather(c, c_parts, 0.25)
    t, t_sends = spread(jnp.concatenate([a, c, b], axis=-1), j, NZ // 2, 0)
    t, t_sends = together((t, t_sends))
    t_parts = [along_z(x, 2 * (k + 1)) for k, x in enumerate(t_sends)]
    core = lax.rem(lax.axis_index("replica"), 2)
    low, high = jnp.where(core == 0, mine, theirs), jnp.where(core == 0, theirs, mine)
    return gather(t, t_parts, 0.25), jnp.concatenate([low, high], axis=0)


def on_device(global_frag, local_frag, outer_mom, grads, inner_param, inner_m, inner_v):
    f = lax.axis_index("fsdp")
    groups = lax.axis_size("fsdp")
    summed, total = sums(grads[0, 0], (global_frag, local_frag[0]), f)
    average = 0.25 * total
    new_mom = 0.9 * outer_mom + average
    new_global = global_frag - 0.7 * (average + 0.9 * new_mom)
    gmean = (summed / groups)[None]
    new_m = 0.9 * inner_m + 0.1 * gmean
    new_v = 0.95 * inner_v + 0.05 * gmean * gmean
    m_hat = new_m / (1.0 - 0.9**STEP)
    v_hat = new_v / (1.0 - 0.95**STEP)
    new_param = inner_param - 0.0003 * (m_hat / (jnp.sqrt(v_hat) + 1e-08) + 0.1 * inner_param)
    return (new_global, new_mom, new_param, new_m, new_v)


def solution(mesh):
    placed = (
        P("fsdp", None),
        P("replica", "fsdp", None),
        P("fsdp", None),
        P("replica", "fsdp", None, None),
        P("replica", "fsdp", None),
        P("replica", "fsdp", None),
        P("replica", "fsdp", None),
    )
    return jax.shard_map(
        on_device,
        mesh=mesh,
        in_specs=placed,
        out_specs=(
            P("fsdp", None),
            P("fsdp", None),
            P("replica", "fsdp", None),
            P("replica", "fsdp", None),
            P("replica", "fsdp", None),
        ),
        check_vma=False,
    )
```

```python
import jax
import jax.numpy as jnp
from jax import lax
from jax.experimental import pallas as pl
from jax.experimental.pallas import tpu as pltpu
from jax.sharding import PartitionSpec as P

BLOCK = 128
STEP = 8
NZ, NY, NH = 8, 4, 2
F32, F16, BF16 = jnp.float32, jnp.float16, jnp.bfloat16
COLS_Y, COLS_H, COLS_Z = 3072, 2560, 2560
FRAG_SCALE = 2048.0


def place(z, y, h):
    return ((z % NZ) * NY + y % NY) * NH + h % NH


def perm_of(step):
    return [
        (place(z, y, h), place(*step(z, y, h)))
        for z in range(NZ)
        for y in range(NY)
        for h in range(NH)
    ]


def along_y(x, k):
    return lax.ppermute(x, "fsdp", perm_of(lambda z, y, h: (z, y + k, h)))


def along_h(x):
    return lax.ppermute(x, "fsdp", perm_of(lambda z, y, h: (z, y, h + 1)))


def along_z(x, k):
    return lax.ppermute(x, "fsdp", perm_of(lambda z, y, h: (z + k, y, h)))


def pair_z(x, shift):
    return lax.ppermute(
        x, "fsdp", perm_of(lambda z, y, h: ((((z + shift) % NZ) ^ 1) - shift, y, h))
    )


def swap_core(x):
    return lax.ppermute(x, "replica", [(0, 1), (1, 0), (2, 3), (3, 2)])


def take(x, index, axis):
    return lax.dynamic_index_in_dim(x, index, axis, keepdims=False)


def rows_of(x, h, axis):
    low = lax.slice_in_dim(x, 0, 4, axis=axis)
    high = lax.slice_in_dim(x, 4, 8, axis=axis)
    return jnp.where(h == 0, low, high)


def spread(x, me, size, axis):
    others = [take(x, lax.rem(me + k, size), axis).astype(F16) for k in range(1, size)]
    return take(x, me, axis), others


def gather(x, parts, factor):
    for part in parts:
        x = x + part.astype(F32)
    return x * factor


def decode(g, l, mine, theirs):
    core = lax.rem(lax.axis_index("replica"), 2)
    half = g.shape[0] // 2
    for i in range(g.shape[1] // BLOCK):
        at = slice(i * BLOCK, (i + 1) * BLOCK)
        delta = g[:, at] - l[:, at]
        amax = jnp.max(jnp.abs(delta), axis=1, keepdims=True)
        scale = ((amax + 1e-06) / 448.0).astype(BF16).astype(F32)
        decoded = (delta / scale) * scale
        low, high = decoded[:half], decoded[half:]
        mine[:, at] = jnp.where(core == 0, low, high)
        theirs[:, at] = jnp.where(core == 0, high, low)


def deal_kernel(
    g, frag_g, frag_l, a1, a2, a3, a0, c_send, c_own, b_send, b_own, mine_out, theirs_out, *scratch
):
    c_all, c_s, c_o, fg, fl, mine, theirs, a_all, b_all, sems = scratch
    f = lax.axis_index("fsdp")
    y, h, p = lax.rem(f // NH, NY), lax.rem(f, NH), lax.rem(f // (NY * NH), 2)
    first, second = COLS_Y, COLS_Y + COLS_H

    def start(src, dst, i):
        copy = pltpu.make_async_copy(src, dst, sems.at[i])
        copy.start()
        return copy

    fg_in = start(frag_g, fg, 0)
    fl_in = start(frag_l, fl, 1)
    a_in = [start(g.at[:, :, lax.rem(y + k, NY), :, :first], a_all.at[k], 2 + k) for k in range(NY)]
    b_in = [start(g.at[:, q, :, :, second:], b_all.at[i], 6 + i) for i, q in enumerate((1 - p, p))]
    c_in = start(g.at[:, :, :, :, first:second], c_all, 8)
    fg_in.wait()
    fl_in.wait()
    decode(fg, fl, mine, theirs)
    dealt = [start(mine, mine_out, 9), start(theirs, theirs_out, 10)]
    for k, out in enumerate((a0, a1, a2, a3)):
        a_in[k].wait()
        dealt.append(start(a_all.at[k], out, 11 + k))
    for i, out in enumerate((b_send, b_own)):
        b_in[i].wait()
        dealt.append(start(b_all.at[i], out, 15 + i))
    c_in.wait()
    for i in range(NZ // 2):
        for q in range(2):
            for j in range(NY):
                low, high = c_all[i, q, j, 0:4, :], c_all[i, q, j, 4:8, :]
                c_s[i, q, j] = jnp.where(h == 0, high, low)
                c_o[i, q, j] = jnp.where(h == 0, low, high)
    dealt.append(start(c_s, c_send, 17))
    dealt.append(start(c_o, c_own, 18))
    for copy in dealt:
        copy.wait()


def deal(g, frag_g, frag_l):
    rows, width = frag_g.shape
    a = jax.ShapeDtypeStruct((NZ // 2, 2, 8, COLS_Y), BF16)
    b = jax.ShapeDtypeStruct((NZ // 2, NY, 8, COLS_Z), BF16)
    c = jax.ShapeDtypeStruct((NZ // 2, 2, NY, 4, COLS_H), BF16)
    half = jax.ShapeDtypeStruct((rows // 2, width), F32)
    anywhere = pl.BlockSpec(memory_space=pl.ANY)
    hbm = pl.BlockSpec(memory_space=pltpu.HBM)
    return pl.pallas_call(
        deal_kernel,
        out_shape=(a, a, a, a, c, c, b, b, half, half),
        in_specs=[hbm] * 3,
        out_specs=(anywhere,) * 10,
        scratch_shapes=[
            pltpu.VMEM((NZ // 2, 2, NY, 8, COLS_H), BF16),
            pltpu.VMEM((NZ // 2, 2, NY, 4, COLS_H), BF16),
            pltpu.VMEM((NZ // 2, 2, NY, 4, COLS_H), BF16),
            pltpu.VMEM((rows, width), F32),
            pltpu.VMEM((rows, width), F32),
            pltpu.VMEM((rows // 2, width), F32),
            pltpu.VMEM((rows // 2, width), F32),
            pltpu.VMEM((NY, NZ // 2, 2, 8, COLS_Y), BF16),
            pltpu.VMEM((2, NZ // 2, NY, 8, COLS_Z), BF16),
            pltpu.SemaphoreType.DMA((19,)),
        ],
        compiler_params=pltpu.CompilerParams(vmem_limit_bytes=18 << 20),
        cost_estimate=pl.CostEstimate(
            flops=8 * rows * width, bytes_accessed=12 << 20, transcendentals=0
        ),
    )(*(pltpu.with_memory_space_constraint(x, pltpu.HBM) for x in (g, frag_g, frag_l)))


def merge_kernel(a0, a1, a2, a3, b_own, b_part, c_own, c_part, a, b, c):
    for i in range(NZ // 2):
        for q in range(2):
            total = a0[i, q].astype(F32)
            for part in (a1, a2, a3):
                total = total + part[i, q].astype(F32)
            a[i, q] = total * 16.0
            for j in range(NY):
                c[i, q, j] = (c_own[i, q, j].astype(F32) + c_part[i, q, j].astype(F32)) * 32.0
        for j in range(NY):
            b[i, j] = (b_own[i, j].astype(F32) + b_part[i, j].astype(F32)) * 32.0


def merge(*parts):
    in_vmem = pl.BlockSpec(memory_space=pltpu.VMEM)
    shapes = [parts[i].shape for i in (0, 4, 6)]
    return pl.pallas_call(
        merge_kernel,
        out_shape=tuple(jax.ShapeDtypeStruct(shape, F32) for shape in shapes),
        in_specs=[in_vmem] * 8,
        out_specs=(in_vmem,) * 3,
        compiler_params=pltpu.CompilerParams(vmem_limit_bytes=20 << 20),
        cost_estimate=pl.CostEstimate(flops=2 << 20, bytes_accessed=8 << 20, transcendentals=0),
    )(*parts)


def sums(g, frag, f):
    z, y, h = f // (NY * NH), (f // NH) % NY, f % NH
    p, j = z % 2, z // 2
    a1, a2, a3, a0, c_send, c_own, b_send, b_own, mine, theirs = deal(
        g.reshape(NZ // 2, 2, NY, 8, g.shape[-1]), *frag
    )
    together = lax.optimization_barrier
    a_parts = [along_y(a2, 2), along_y(a1, 1), along_y(a3, 3)]
    c_part = along_h(c_send)
    b_part = pair_z(b_send, 0)
    near = swap_core(theirs)
    pair = ((mine + near) * FRAG_SCALE).astype(F16)
    a0, c_own, b_own, a_parts, c_part, b_part = together(
        (a0, c_own, b_own, a_parts, c_part, b_part)
    )
    a, b, c = merge(a0, *a_parts, b_own, b_part, c_own, c_part)
    a, a_send = rows_of(a, h, 2), rows_of(a, 1 - h, 2).astype(F16)
    b, b_sends = spread(b, y, NY, 1)
    c, c_send = take(c, p, 1), take(c, 1 - p, 1).astype(F16)
    a, a_send, b, b_sends, c, c_send = together((a, a_send, b, b_sends, c, c_send))
    b_parts = [along_y(b_sends[k - 1], k) for k in (2, 1, 3)]
    a_part = along_h(a_send)
    far = lax.ppermute(pair, "replica", [(0, 2), (2, 0), (1, 3), (3, 1)])
    c_part = pair_z(c_send, 0)
    a, a_part, b, b_parts, c, c_part, pair, far = together(
        (a, a_part, b, b_parts, c, c_part, pair, far)
    )
    a = (a + a_part.astype(F32)) * 0.5
    b = gather(b, b_parts, 0.25)
    c = (c + c_part.astype(F32)) * 0.5
    mine = (pair.astype(F32) + far.astype(F32)) * (1.0 / FRAG_SCALE)
    a, a_send = take(a, p, 1), take(a, 1 - p, 1).astype(F16)
    b, b_send = rows_of(b, h, 1), rows_of(b, 1 - h, 1).astype(F16)
    c, c_sends = spread(c, y, NY, 1)
    a, a_send, b, b_send, c, c_sends, mine = together(
        (a, a_send, b, b_send, c, c_sends, mine)
    )
    theirs = swap_core(mine)
    c_parts = [along_y(c_sends[k - 1], k) for k in (2, 1, 3)]
    b_part = along_h(b_send)
    a_part = pair_z(a_send, 0)
    a, a_part, b, b_part, c, c_parts, mine, theirs = together(
        (a, a_part, b, b_part, c, c_parts, mine, theirs)
    )
    a = (a + a_part.astype(F32)) * 0.5
    b = (b + b_part.astype(F32)) * 0.5
    c = gather(c, c_parts, 0.25)
    t, t_sends = spread(jnp.concatenate([a, c, b], axis=-1), j, NZ // 2, 0)
    t, t_sends = together((t, t_sends))
    t_parts = [along_z(x, 2 * (k + 1)) for k, x in enumerate(t_sends)]
    core = lax.rem(lax.axis_index("replica"), 2)
    low, high = jnp.where(core == 0, mine, theirs), jnp.where(core == 0, theirs, mine)
    return gather(t, t_parts, 0.25), jnp.concatenate([low, high], axis=0)


def on_device(global_frag, local_frag, outer_mom, grads, inner_param, inner_m, inner_v):
    f = lax.axis_index("fsdp")
    groups = lax.axis_size("fsdp")
    summed, total = sums(grads[0, 0], (global_frag, local_frag[0]), f)
    average = 0.25 * total
    new_mom = 0.9 * outer_mom + average
    new_global = global_frag - 0.7 * (average + 0.9 * new_mom)
    gmean = (summed / groups)[None]
    new_m = 0.9 * inner_m + 0.1 * gmean
    new_v = 0.95 * inner_v + 0.05 * gmean * gmean
    m_hat = new_m / (1.0 - 0.9**STEP)
    v_hat = new_v / (1.0 - 0.95**STEP)
    new_param = inner_param - 0.0003 * (m_hat / (jnp.sqrt(v_hat) + 1e-08) + 0.1 * inner_param)
    return (new_global, new_mom, new_param, new_m, new_v)


def solution(mesh):
    placed = (
        P("fsdp", None),
        P("replica", "fsdp", None),
        P("fsdp", None),
        P("replica", "fsdp", None, None),
        P("replica", "fsdp", None),
        P("replica", "fsdp", None),
        P("replica", "fsdp", None),
    )
    return jax.shard_map(
        on_device,
        mesh=mesh,
        in_specs=placed,
        out_specs=(
            P("fsdp", None),
            P("fsdp", None),
            P("replica", "fsdp", None),
            P("replica", "fsdp", None),
            P("replica", "fsdp", None),
        ),
        check_vma=False,
    )
```

```python
import jax
import jax.numpy as jnp
from jax import lax
from jax.experimental import pallas as pl
from jax.experimental.pallas import tpu as pltpu
from jax.sharding import PartitionSpec as P

BLOCK = 128
STEP = 8
NZ, NY, NH = 8, 4, 2
F32, F16, BF16 = jnp.float32, jnp.float16, jnp.bfloat16
COLS_Y, COLS_H, COLS_Z = 3072, 2560, 2560
FRAG_SCALE = 2048.0


def place(z, y, h):
    return ((z % NZ) * NY + y % NY) * NH + h % NH


def perm_of(step):
    return [
        (place(z, y, h), place(*step(z, y, h)))
        for z in range(NZ)
        for y in range(NY)
        for h in range(NH)
    ]


def along_y(x, k):
    return lax.ppermute(x, "fsdp", perm_of(lambda z, y, h: (z, y + k, h)))


def along_h(x):
    return lax.ppermute(x, "fsdp", perm_of(lambda z, y, h: (z, y, h + 1)))


def along_z(x, k):
    return lax.ppermute(x, "fsdp", perm_of(lambda z, y, h: (z + k, y, h)))


def pair_z(x, shift):
    return lax.ppermute(
        x, "fsdp", perm_of(lambda z, y, h: ((((z + shift) % NZ) ^ 1) - shift, y, h))
    )


def swap_core(x):
    return lax.ppermute(x, "replica", [(0, 1), (1, 0), (2, 3), (3, 2)])


def take(x, index, axis):
    return lax.dynamic_index_in_dim(x, index, axis, keepdims=False)


def rows_of(x, h, axis):
    low = lax.slice_in_dim(x, 0, 4, axis=axis)
    high = lax.slice_in_dim(x, 4, 8, axis=axis)
    return jnp.where(h == 0, low, high)


def spread(x, me, size, axis):
    others = [take(x, lax.rem(me + k, size), axis).astype(F16) for k in range(1, size)]
    return take(x, me, axis), others


def gather(x, parts, factor):
    for part in parts:
        x = x + part.astype(F32)
    return x * factor


def decode(g, l, mine, theirs):
    core = lax.rem(lax.axis_index("replica"), 2)
    half = g.shape[0] // 2
    for i in range(g.shape[1] // BLOCK):
        at = slice(i * BLOCK, (i + 1) * BLOCK)
        delta = g[:, at] - l[:, at]
        amax = jnp.max(jnp.abs(delta), axis=1, keepdims=True)
        scale = ((amax + 1e-06) / 448.0).astype(BF16).astype(F32)
        decoded = (delta / scale) * scale
        low, high = decoded[:half], decoded[half:]
        mine[:, at] = jnp.where(core == 0, low, high)
        theirs[:, at] = jnp.where(core == 0, high, low)


def deal_kernel(
    g, frag_g, frag_l, a1, a2, a3, a0, c_send, c_own, b_send, b_own, mine_out, theirs_out, *scratch
):
    c_all, c_s, c_o, fg, fl, mine, theirs, a_all, b_all, sems = scratch
    f = lax.axis_index("fsdp")
    y, h, p = lax.rem(f // NH, NY), lax.rem(f, NH), lax.rem(f // (NY * NH), 2)
    first, second = COLS_Y, COLS_Y + COLS_H

    def start(src, dst, i):
        copy = pltpu.make_async_copy(src, dst, sems.at[i])
        copy.start()
        return copy

    fg_in = start(frag_g, fg, 0)
    fl_in = start(frag_l, fl, 1)
    a_in = [start(g.at[:, :, lax.rem(y + k, NY), :, :first], a_all.at[k], 2 + k) for k in range(NY)]
    b_in = [start(g.at[:, q, :, :, second:], b_all.at[i], 6 + i) for i, q in enumerate((1 - p, p))]
    c_in = start(g.at[:, :, :, :, first:second], c_all, 8)
    fg_in.wait()
    fl_in.wait()
    decode(fg, fl, mine, theirs)
    dealt = [start(mine, mine_out, 9), start(theirs, theirs_out, 10)]
    for k, out in enumerate((a0, a1, a2, a3)):
        a_in[k].wait()
        dealt.append(start(a_all.at[k], out, 11 + k))
    for i, out in enumerate((b_send, b_own)):
        b_in[i].wait()
        dealt.append(start(b_all.at[i], out, 15 + i))
    c_in.wait()
    for i in range(NZ // 2):
        for q in range(2):
            for j in range(NY):
                low, high = c_all[i, q, j, 0:4, :], c_all[i, q, j, 4:8, :]
                c_s[i, q, j] = jnp.where(h == 0, high, low)
                c_o[i, q, j] = jnp.where(h == 0, low, high)
    dealt.append(start(c_s, c_send, 17))
    dealt.append(start(c_o, c_own, 18))
    for copy in dealt:
        copy.wait()


def deal(g, frag_g, frag_l):
    rows, width = frag_g.shape
    a = jax.ShapeDtypeStruct((NZ // 2, 2, 8, COLS_Y), BF16)
    b = jax.ShapeDtypeStruct((NZ // 2, NY, 8, COLS_Z), BF16)
    c = jax.ShapeDtypeStruct((NZ // 2, 2, NY, 4, COLS_H), BF16)
    half = jax.ShapeDtypeStruct((rows // 2, width), F32)
    anywhere = pl.BlockSpec(memory_space=pl.ANY)
    hbm = pl.BlockSpec(memory_space=pltpu.HBM)
    return pl.pallas_call(
        deal_kernel,
        out_shape=(a, a, a, a, c, c, b, b, half, half),
        in_specs=[hbm] * 3,
        out_specs=(anywhere,) * 10,
        scratch_shapes=[
            pltpu.VMEM((NZ // 2, 2, NY, 8, COLS_H), BF16),
            pltpu.VMEM((NZ // 2, 2, NY, 4, COLS_H), BF16),
            pltpu.VMEM((NZ // 2, 2, NY, 4, COLS_H), BF16),
            pltpu.VMEM((rows, width), F32),
            pltpu.VMEM((rows, width), F32),
            pltpu.VMEM((rows // 2, width), F32),
            pltpu.VMEM((rows // 2, width), F32),
            pltpu.VMEM((NY, NZ // 2, 2, 8, COLS_Y), BF16),
            pltpu.VMEM((2, NZ // 2, NY, 8, COLS_Z), BF16),
            pltpu.SemaphoreType.DMA((19,)),
        ],
        compiler_params=pltpu.CompilerParams(vmem_limit_bytes=18 << 20),
        cost_estimate=pl.CostEstimate(
            flops=8 * rows * width, bytes_accessed=12 << 20, transcendentals=0
        ),
    )(*(pltpu.with_memory_space_constraint(x, pltpu.HBM) for x in (g, frag_g, frag_l)))


def merge_kernel(a0, a1, a2, a3, b_own, b_part, c_own, c_part, a, b, c):
    for i in range(NZ // 2):
        for q in range(2):
            total = a0[i, q].astype(F32)
            for part in (a1, a2, a3):
                total = total + part[i, q].astype(F32)
            a[i, q] = total * 16.0
            for j in range(NY):
                c[i, q, j] = (c_own[i, q, j].astype(F32) + c_part[i, q, j].astype(F32)) * 32.0
        for j in range(NY):
            b[i, j] = (b_own[i, j].astype(F32) + b_part[i, j].astype(F32)) * 32.0


def merge(*parts):
    in_vmem = pl.BlockSpec(memory_space=pltpu.VMEM)
    shapes = [parts[i].shape for i in (0, 4, 6)]
    return pl.pallas_call(
        merge_kernel,
        out_shape=tuple(jax.ShapeDtypeStruct(shape, F32) for shape in shapes),
        in_specs=[in_vmem] * 8,
        out_specs=(in_vmem,) * 3,
        compiler_params=pltpu.CompilerParams(vmem_limit_bytes=20 << 20),
        cost_estimate=pl.CostEstimate(flops=2 << 20, bytes_accessed=8 << 20, transcendentals=0),
    )(*parts)


def sums(g, frag, f):
    z, y, h = f // (NY * NH), (f // NH) % NY, f % NH
    p, j = z % 2, z // 2
    a1, a2, a3, a0, c_send, c_own, b_send, b_own, mine, theirs = deal(
        g.reshape(NZ // 2, 2, NY, 8, g.shape[-1]), *frag
    )
    together = lax.optimization_barrier
    a_parts = [along_y(a2, 2), along_y(a1, 1), along_y(a3, 3)]
    c_part = along_h(c_send)
    b_part = pair_z(b_send, 0)
    near = swap_core(theirs)
    pair = ((mine + near) * FRAG_SCALE).astype(F16)
    a0, c_own, b_own, a_parts, c_part, b_part = together(
        (a0, c_own, b_own, a_parts, c_part, b_part)
    )
    a, b, c = merge(a0, *a_parts, b_own, b_part, c_own, c_part)
    a, a_send = rows_of(a, h, 2), rows_of(a, 1 - h, 2).astype(F16)
    b, b_sends = spread(b, y, NY, 1)
    c, c_send = take(c, p, 1), take(c, 1 - p, 1).astype(F16)
    a, a_send, b, b_sends, c, c_send = together((a, a_send, b, b_sends, c, c_send))
    b_parts = [along_y(b_sends[k - 1], k) for k in (2, 1, 3)]
    a_part = along_h(a_send)
    far = lax.ppermute(pair, "replica", [(0, 2), (2, 0), (1, 3), (3, 1)])
    c_part = pair_z(c_send, 0)
    a, a_part, b, b_parts, c, c_part, pair, far = together(
        (a, a_part, b, b_parts, c, c_part, pair, far)
    )
    a = (a + a_part.astype(F32)) * 0.5
    b = gather(b, b_parts, 0.25)
    c = (c + c_part.astype(F32)) * 0.5
    mine = (pair.astype(F32) + far.astype(F32)) * (1.0 / FRAG_SCALE)
    a, a_send = take(a, p, 1), take(a, 1 - p, 1).astype(F16)
    b, b_send = rows_of(b, h, 1), rows_of(b, 1 - h, 1).astype(F16)
    c, c_sends = spread(c, y, NY, 1)
    a, a_send, b, b_send, c, c_sends, mine = together(
        (a, a_send, b, b_send, c, c_sends, mine)
    )
    theirs = swap_core(mine)
    c_parts = [along_y(c_sends[k - 1], k) for k in (2, 1, 3)]
    b_part = along_h(b_send)
    a_part = pair_z(a_send, 0)
    a, a_part, b, b_part, c, c_parts, mine, theirs = together(
        (a, a_part, b, b_part, c, c_parts, mine, theirs)
    )
    a = (a + a_part.astype(F32)) * 0.5
    b = (b + b_part.astype(F32)) * 0.5
    c = gather(c, c_parts, 0.25)
    t, t_sends = spread(jnp.concatenate([a, c, b], axis=-1), j, NZ // 2, 0)
    t, t_sends = together((t, t_sends))
    t_parts = [along_z(t_sends[k - 1], 2 * k) for k in (1, 3, 2)]
    core = lax.rem(lax.axis_index("replica"), 2)
    low, high = jnp.where(core == 0, mine, theirs), jnp.where(core == 0, theirs, mine)
    return gather(t, t_parts, 0.25), jnp.concatenate([low, high], axis=0)


def on_device(global_frag, local_frag, outer_mom, grads, inner_param, inner_m, inner_v):
    f = lax.axis_index("fsdp")
    groups = lax.axis_size("fsdp")
    summed, total = sums(grads[0, 0], (global_frag, local_frag[0]), f)
    average = 0.25 * total
    new_mom = 0.9 * outer_mom + average
    new_global = global_frag - 0.7 * (average + 0.9 * new_mom)
    gmean = (summed / groups)[None]
    new_m = 0.9 * inner_m + 0.1 * gmean
    new_v = 0.95 * inner_v + 0.05 * gmean * gmean
    m_hat = new_m / (1.0 - 0.9**STEP)
    v_hat = new_v / (1.0 - 0.95**STEP)
    new_param = inner_param - 0.0003 * (m_hat / (jnp.sqrt(v_hat) + 1e-08) + 0.1 * inner_param)
    return (new_global, new_mom, new_param, new_m, new_v)


def solution(mesh):
    placed = (
        P("fsdp", None),
        P("replica", "fsdp", None),
        P("fsdp", None),
        P("replica", "fsdp", None, None),
        P("replica", "fsdp", None),
        P("replica", "fsdp", None),
        P("replica", "fsdp", None),
    )
    return jax.shard_map(
        on_device,
        mesh=mesh,
        in_specs=placed,
        out_specs=(
            P("fsdp", None),
            P("fsdp", None),
            P("replica", "fsdp", None),
            P("replica", "fsdp", None),
            P("replica", "fsdp", None),
        ),
        check_vma=False,
    )
```
